256 devices in a mesh: seed: 4 (over x), fsdp: 8 (over y, core), seq: 8 (over z).
Axes of the slice: x: 4, y: 4, z: 8, core: 2. Of those that a mesh axis runs over, the one named last changes fastest.
Arguments:
- mel_frames: bfloat16 [8, 32768, 80], P('fsdp', 'seq'), may hold values from -6 to 6
- lengths: int32 [8], P('fsdp'), may hold values from 1 to 8192, 40960 in all
- targets: int32 [8, 8192], P('fsdp', 'seq'), may hold values from 0 to 511
- frame_mask: int32 [8, 8192], P('fsdp', 'seq'), may hold values 0 or 1
- stem_weight: bfloat16 [4, 640, 1536], P('seed'), may hold values from -0.25 to 0.25
- conv_in_weight: bfloat16 [4, 1536, 1536], P('seed', ('fsdp', 'seq')), may hold values from -0.15625 to 0.15625
- conv_out_weight: bfloat16 [4, 768, 1536], P('seed', ('fsdp', 'seq')), may hold values from -0.21875 to 0.21875
- depth_weight: bfloat16 [4, 31, 768], P('seed'), may hold values from -1 to 1
- head_weight: bfloat16 [4, 1536, 512], P('seed', ('fsdp', 'seq')), may hold values from -80 to 80
- norm_gain: float32 [4, 2, 1536], P('seed'), may hold values from 0.5 to 1.5
Outputs:
- frame_error: float32 [8, 8192], P('fsdp', 'seq')
- utt_score: float32 [8], P('fsdp')
The draws below stay inside these ranges and needn't reach their ends.
Inputs may be any that keep to these rules, and one draw needn't show every extreme that they name: `lengths`: some utterance has exactly 8192 valid frames.
All inputs are finite; a program needn't handle non-finite values. No bound on the sum of `lengths` or of `frame_mask` on one device may be relied on, other than what follows from the above.
Results may differ from the reference program's by a relative error of at most 0.0022.
Values may be sent and summed in bfloat16 or wider, within the bound.
A program may use at most 64 MiB of HBM per device.

```python
import math
import jax
import jax.numpy as jnp
import numpy as np
from jax import lax

D = 1536
CONV = 768
VOCAB = 512
MELS = 80
KERNEL = 31
SEEDS = 4
UTTS = 8
FRAMES = 8192
MEL_FRAMES = 32768
N_FSDP = 8


def draw_head_weight(key, part):
    base_key = jax.random.fold_in(key, 0)
    shape = (SEEDS, D, VOCAB)
    base = jax.random.truncated_normal(base_key, -4.0, 4.0, shape, jnp.float32)
    weight = base * (3.0 / math.sqrt(D))
    return weight.astype(jnp.bfloat16)


def with_ends(values, key, least, top_value):
    shape = values.shape
    index_at = [jax.random.randint(jax.random.fold_in(key, axis), (), 0, shape[axis]) for axis in range(len(shape))]
    values = values.at[tuple(index_at)].set(least)
    longest = shape.index(max(shape))
    index_at[longest] = (index_at[longest] + 1) % shape[longest]
    return values.at[tuple(index_at)].set(top_value)


def levels(key, dims, cuts, low, high):
    loudness = 1.0
    for dim, blocks in cuts:
        draws = jax.random.uniform(jax.random.fold_in(jax.random.fold_in(key, 6), dim), (blocks,), jnp.float32, low / len(cuts), high / len(cuts))
        loudness = loudness * jnp.repeat(jnp.exp(draws), dims[dim] // blocks).reshape((-1,) + (1,) * (len(dims) - 1 - dim))
    return loudness


def split_up(number_of, total, bound, skew):
    loads = [(1 << 20) // math.isqrt(rank ** skew) + 1 for rank in range(2, number_of + 1)]
    spare, counts = total - bound - (number_of - 1), [1] * (number_of - 1)
    while spare > 0:
        free = [i for i in range(number_of - 1) if counts[i] < bound]
        mass, remaining = sum([loads[i] for i in free]), spare
        for i in free:
            extra = min(bound - counts[i], max(1, remaining * loads[i] // mass), spare)
            counts[i] = counts[i] + extra
            spare = spare - extra
    return np.array([bound] + counts)


def ragged(own_key, number_of, total, most, lean):
    if number_of == 2:
        one = jax.random.randint(own_key, (), max(1, total - most), min(most, total - 1) + 1)
        return jnp.stack([one, total - one])
    tallies = jnp.asarray(split_up(number_of, total, most, lean), jnp.int32)
    pairs = (number_of - 1) // 2
    source_of, receiver = tallies[1:1 + 2 * pairs:2], tallies[2:2 + 2 * pairs:2]
    slack = jnp.minimum(source_of - 1, most - receiver)
    moved = jax.random.randint(jax.random.fold_in(own_key, 1), (pairs,), 0, 1 << 20) % (slack + 1)
    tallies = tallies.at[1:1 + 2 * pairs:2].set(source_of - moved).at[2:2 + 2 * pairs:2].set(receiver + moved)
    return tallies[jax.random.permutation(jax.random.fold_in(own_key, 2), number_of)]


def noise(rng, shape, scale, bound, shards=(), dtype=jnp.bfloat16):
    factor_of = levels(rng, shape, shards, -0.22, 0.18) if shards else 1.0
    values = jax.random.normal(rng, shape, jnp.float32) * scale * factor_of
    return jnp.minimum(jnp.maximum(values, -bound), bound).astype(dtype)


def setup_inputs(seed: int = 0) -> dict:
    arg_keys = jax.random.split(jax.random.key(seed), 11)
    mel_frames = noise(arg_keys[0], (UTTS, MEL_FRAMES, MELS), 1.0, 6.0, ((0, 8), (1, 8)))
    lengths = ragged(arg_keys[1], UTTS, N_FSDP * FRAMES * 5 // 8, FRAMES, 2).astype(jnp.int32)
    targets = with_ends(jax.random.randint(arg_keys[2], (UTTS, FRAMES), 0, VOCAB), jax.random.fold_in(arg_keys[2], 1), 0, VOCAB - 1).astype(jnp.int32)
    frame_mask = with_ends((jax.random.randint(arg_keys[3], (UTTS, FRAMES), 0, 8) < 7).astype(jnp.int32), jax.random.fold_in(arg_keys[3], 1), 0, 1)
    stem_weight = noise(arg_keys[4], (SEEDS, 8 * MELS, D), (8 * MELS) ** -0.5, 0.25, ((0, 4),))
    conv_in_weight = noise(arg_keys[5], (SEEDS, D, 2 * CONV), D ** -0.5, 0.15625, ((0, 4), (1, 64)))
    conv_out_weight = noise(arg_keys[6], (SEEDS, CONV, D), CONV ** -0.5, 0.21875, ((0, 4), (1, 64)))
    depth_weight = noise(arg_keys[7], (SEEDS, KERNEL, CONV), KERNEL ** -0.5, 1.0, ((0, 4),))
    head_weight = draw_head_weight(jax.random.fold_in(arg_keys[10], 71), 0)
    norm_gain = jnp.clip(1.0 + 0.1 * jax.random.normal(arg_keys[9], (SEEDS, 2, D), jnp.float32), 0.5, 1.5)
    return {"mel_frames": mel_frames, "lengths": lengths, "targets": targets, "frame_mask": frame_mask, "stem_weight": stem_weight, "conv_in_weight": conv_in_weight, "conv_out_weight": conv_out_weight, "depth_weight": depth_weight, "head_weight": head_weight, "norm_gain": norm_gain}


def layer_norm(values, gain_row):
    row_mean = lax.optimization_barrier(jnp.mean(values, axis=-1, keepdims=True))
    centred = values - row_mean
    row_var = lax.optimization_barrier(jnp.mean(centred * centred, axis=-1, keepdims=True))
    return (centred * lax.rsqrt(row_var + 1e-05) * gain_row).astype(jnp.bfloat16)

def utterance(weights, mel_block, length, target_ids, mask_row):
    stem_matrix, gate_matrix, back_matrix, depth_taps, head_matrix, gain_rows = weights
    frame_count = target_ids.shape[0]
    blocks = mel_block.reshape(frame_count, -1)
    following = jnp.concatenate([blocks[1:], jnp.zeros_like(blocks[:1])], 0)
    half_width = blocks.shape[1]
    stem_out = (jnp.dot(blocks, stem_matrix[:half_width], preferred_element_type=jnp.float32) + jnp.dot(following, stem_matrix[half_width:], preferred_element_type=jnp.float32)).astype(jnp.bfloat16)
    positions = jnp.arange(frame_count).astype(jnp.int32)
    frame_live = positions < length
    live_column = frame_live[:, None].astype(jnp.float32)
    normed_one = layer_norm(stem_out.astype(jnp.float32), gain_rows[0])
    mixed_rows = jnp.dot(normed_one, gate_matrix, preferred_element_type=jnp.float32)
    gated_rows = (mixed_rows[:, :CONV] * jax.nn.sigmoid(mixed_rows[:, CONV:]) * live_column).astype(jnp.bfloat16)
    halo_width = KERNEL // 2
    padded = jnp.pad(gated_rows, ((halo_width, halo_width), (0, 0)))
    depthwise = jnp.zeros((frame_count, CONV), jnp.float32)
    for tap_index in range(KERNEL):
        depthwise = depthwise + padded[tap_index:tap_index + frame_count].astype(jnp.float32) * depth_taps[tap_index].astype(jnp.float32)
    swished = jax.nn.silu(depthwise).astype(jnp.bfloat16)
    after_conv = stem_out.astype(jnp.float32) + jnp.dot(swished, back_matrix, preferred_element_type=jnp.float32)
    normed_two = layer_norm(after_conv, gain_rows[1])
    logits = jnp.dot(normed_two, head_matrix, preferred_element_type=jnp.float32)
    posterior = jax.nn.softmax(logits, axis=-1)
    onehot = (jnp.arange(logits.shape[1]).astype(jnp.int32)[None, :] == target_ids[:, None]).astype(jnp.float32)
    differ = posterior - onehot
    frame_err = jnp.sqrt(lax.optimization_barrier(jnp.sum(differ * differ, axis=-1)))
    return frame_err * frame_live.astype(jnp.float32) * mask_row.astype(jnp.float32)

def reference(mel_frames, lengths, targets, frame_mask, stem_weight, conv_in_weight, conv_out_weight, depth_weight, head_weight, norm_gain):

    def per_seed(seed_index):
        weights = (stem_weight[seed_index], conv_in_weight[seed_index], conv_out_weight[seed_index], depth_weight[seed_index], head_weight[seed_index], norm_gain[seed_index])

        def per_utt(utt_index):
            return utterance(weights, mel_frames[utt_index], lengths[utt_index], targets[utt_index], frame_mask[utt_index])
        return lax.map(per_utt, jnp.arange(UTTS).astype(jnp.int32))
    errors = lax.map(per_seed, jnp.arange(SEEDS).astype(jnp.int32))
    frame_error = lax.optimization_barrier(jnp.sum(errors, axis=0)) / jnp.float32(SEEDS)
    utt_score = lax.optimization_barrier(jnp.sum(frame_error, axis=-1)) / lengths.astype(jnp.float32)
    return (frame_error, utt_score)
```

```python
import functools

import jax
import jax.numpy as jnp
from jax import lax
from jax.experimental import pallas as pl
from jax.experimental.pallas import tpu as pltpu
from jax.sharding import PartitionSpec as P

MESH = pl.DeviceIdType.MESH
F32 = jnp.float32
BF16 = jnp.bfloat16
HALO = 16
TAIL = 80
LANES = 128
GROUP = 256
GROUPS = 3
Y, CORES, Z, X = 4, 2, 8, 4


class Piece:
    def __init__(self, place, own, dst, send, recv, local, y_first, flip):
        self.place, self.own, self.dst = place, own, dst
        self.send, self.recv, self.local = send, recv, local
        self.y_first, self.flip = y_first, flip
        self.used = 0
        self.copies = []
        self.pending = []
        self.round = 0

    def remote(self, src, dst, device):
        slot = self.used
        self.used += 1
        copy = pltpu.make_async_remote_copy(
            src_ref=src,
            dst_ref=dst,
            send_sem=self.send.at[slot],
            recv_sem=self.recv.at[slot],
            device_id=device,
            device_id_type=MESH,
        )
        copy.start()
        self.copies.append(copy)
        self.pending.append(copy)

    def at_z(self, by):
        x, y, c, z = self.place
        return (x, y * CORES + c, lax.rem(z + by + Z, Z))

    def at_y(self, by):
        x, y, c, z = self.place
        return (x, lax.rem(y + by + Y, Y) * CORES + c, z)

    def z_step(self, step):
        x, y, c, z = self.place
        for sign in (1, -1):
            if step == 4 and sign == (1 if self.flip else -1):
                continue
            owner = lax.rem(z - sign * (step - 1) + Z, Z)
            if self.y_first:
                block = self.dst.at[:, c, owner]
                self.remote(block, block, self.at_z(sign))
            else:
                block = self.dst.at[y, c, owner]
                self.remote(self.own if step == 1 else block, block, self.at_z(sign))

    def y_step(self):
        x, y, c, z = self.place
        block = self.dst.at[y, c, z] if self.y_first else self.dst.at[y, c]
        for by in (1, 3, 2):
            self.remote(self.own if self.y_first else block, block, self.at_y(by))

    def arrived(self):
        for copy in self.pending:
            copy.wait_recv()
        self.pending = []

    def step(self):
        x, y, c, z = self.place
        now = self.round
        self.round += 1
        if now == 0:
            keep = pltpu.make_async_copy(self.own, self.dst.at[y, c, z], self.local)
            if self.y_first:
                self.y_step()
            else:
                self.z_step(1)
            keep.start()
            self.keep = keep
            return
        self.arrived()
        if now == 1:
            self.keep.wait()
        if now <= 4:
            if self.y_first:
                self.z_step(now)
            elif now <= 3:
                self.z_step(now + 1)
            else:
                self.y_step()
        elif now == 5:
            block = self.dst.at[:, c]
            self.remote(block, block, (x, y * CORES + 1 - c, z))

    def finish(self):
        for copy in self.copies:
            copy.wait_send()


def normalised(values, gain_row):
    row_mean = jnp.mean(values, axis=-1, keepdims=True)
    centred = values - row_mean
    row_var = jnp.mean(centred * centred, axis=-1, keepdims=True)
    return (centred * lax.rsqrt(row_var + 1e-05) * gain_row).astype(BF16)


def dot(left, right):
    return jnp.dot(left, right, preferred_element_type=F32)


def kernel(
    rows,
    taps,
    lengths_ref,
    targets_ref,
    mask_ref,
    gain_ref,
    depth_ref,
    mel_hbm,
    stem_hbm,
    gate_hbm,
    back_hbm,
    head_hbm,
    error_ref,
    score_ref,
    mel_bf,
    mel_f32,
    stem_w,
    gate_a,
    gate_b,
    back_a,
    back_b,
    head_a,
    head_b,
    back_w,
    stem_out,
    normed,
    gated,
    swished,
    tap_rows,
    square,
    error_cols,
    seed_parts,
    seq_parts,
    send_sem,
    recv_sem,
    local_sem,
    mel_send,
    mel_recv,
    out_send,
    out_recv,
):
    x = lax.axis_index("seed")
    fsdp = lax.axis_index("fsdp")
    y, c = fsdp // CORES, lax.rem(fsdp, CORES)
    z = lax.axis_index("seq")
    place = (x, y, c, z)
    wide = rows + 2 * HALO
    channels = GROUP * GROUPS

    barrier = pltpu.get_barrier_semaphore()
    peers = [(x, fsdp, lax.rem(z + d, Z)) for d in range(1, Z)]
    peers += [(x, lax.rem(y + d, Y) * CORES + c, z) for d in range(1, Y)]
    peers += [(lax.rem(x + d, X), fsdp, z) for d in range(1, X)]
    peers += [(x, y * CORES + 1 - c, z)]
    for peer in peers:
        pl.semaphore_signal(barrier, inc=1, device_id=peer, device_id_type=MESH)

    mel_rows = 4 * rows
    loads = [
        pltpu.make_async_copy(mel_hbm.at[0], mel_bf.at[pl.ds(4 * HALO, mel_rows)], local_sem.at[10]),
        pltpu.make_async_copy(stem_hbm.at[0], stem_w, local_sem.at[11]),
    ]
    for load in loads:
        load.start()

    specs = []
    for group in range(GROUPS):
        specs.append((gate_hbm, GROUP * group, GROUP, gate_a.at[group], False))
        specs.append((gate_hbm, channels + GROUP * group, GROUP, gate_b.at[group], True))
    half = back_hbm.shape[2] // 2
    specs.append((back_hbm, 0, half, back_a, False))
    specs.append((back_hbm, half, half, back_b, True))
    quarter = head_hbm.shape[2] // 2
    specs.append((head_hbm, 0, quarter, head_a, False))
    specs.append((head_hbm, quarter, quarter, head_b, True))
    pieces = []
    for index, (source, start, width, dst, y_first) in enumerate(specs):
        own = source.at[0, :, pl.ds(start, width)]
        pieces.append(
            Piece(place, own, dst, send_sem.at[index], recv_sem.at[index], local_sem.at[index], y_first, index % 4 >= 2)
        )
    starts = (0, 0, 1, 1, 2, 2, 3, 3, 4, 4)

    def comm(now):
        for piece, start in zip(pieces, starts):
            if start <= now <= start + 6:
                piece.step()

    pl.semaphore_wait(barrier, len(peers))
    comm(0)
    halo = [
        pltpu.make_async_remote_copy(
            src_ref=mel_hbm.at[0, pl.ds(mel_rows - 4 * HALO, 4 * HALO)],
            dst_ref=mel_bf.at[pl.ds(0, 4 * HALO)],
            send_sem=mel_send.at[0],
            recv_sem=mel_recv.at[0],
            device_id=(x, fsdp, lax.rem(z + 1, Z)),
            device_id_type=MESH,
        ),
        pltpu.make_async_remote_copy(
            src_ref=mel_hbm.at[0, pl.ds(0, TAIL)],
            dst_ref=mel_bf.at[pl.ds(4 * HALO + mel_rows, TAIL)],
            send_sem=mel_send.at[1],
            recv_sem=mel_recv.at[1],
            device_id=(x, fsdp, lax.rem(z + Z - 1, Z)),
            device_id_type=MESH,
        ),
    ]
    for copy in halo:
        copy.start()

    length = lengths_ref[0]
    tap_rows[...] = jnp.zeros_like(tap_rows)
    tap_rows[1 : 1 + taps, :] = depth_ref[0].astype(F32)
    square[...] = jnp.zeros_like(square)
    blocks = rows // LANES
    for b in range(blocks):
        square[b : b + 1, :] = targets_ref[0:1, b * LANES : (b + 1) * LANES].astype(F32)
    square[...] = square[...].T

    for load in loads:
        load.wait()
    for copy in halo:
        copy.wait_recv()
    comm(1)

    mel_f32[: 4 * HALO + mel_rows, :] = mel_bf[: 4 * HALO + mel_rows, :].astype(F32)
    more = (z < Z - 1).astype(F32)
    mel_f32[4 * HALO + mel_rows :, :] = mel_bf[4 * HALO + mel_rows :, :].astype(F32) * more
    tall = wide // 3

    def stem(part):
        r0 = part * tall
        window = [mel_f32[pl.ds(4 * r0 + i, tall, stride=4), :] for i in range(8)]
        frames = jnp.concatenate(window, axis=1).astype(BF16)
        out = dot(frames, stem_w[...]).astype(BF16)
        stem_out[r0 : r0 + tall, :] = out
        normed[r0 : r0 + tall, :] = normalised(out.astype(F32), gain_ref[0, 0:1, :])

    for part in range(3):
        stem(part)
        comm(2 + part)
    comm(5)
    comm(6)

    def gate(group):
        @pl.loop(0, 3)
        def _(part):
            r0 = pl.multiple_of(part * tall, 16)
            left = normed[pl.ds(r0, tall), :]
            value = dot(left, gate_a[group].reshape(-1, GROUP))
            control = dot(left, gate_b[group].reshape(-1, GROUP))
            position = z * rows - HALO + r0 + lax.broadcasted_iota(jnp.int32, (tall, 1), 0)
            live = jnp.where((position >= 0) & (position < length), 1.0, 0.0).astype(F32)
            result = (value * jax.nn.sigmoid(control) * live).astype(BF16).astype(F32)
            for k in range(GROUP // LANES):
                gated[k, pl.ds(r0, tall), :] = result[:, k * LANES : (k + 1) * LANES]

    def depthwise(group, first, last):
        size = 64

        @pl.loop(first, last)
        def _(part):
            r0 = pl.multiple_of(part * size, size)
            for k in range(GROUP // LANES):
                column = group * GROUP + k * LANES
                around = gated[k, pl.ds(r0, size + 32), :]
                total = jnp.zeros((size, LANES), F32)
                for s in range(8):
                    partial = None
                    for a in range(4):
                        if a == 0 and s == 0:
                            continue
                        term = around[8 * a : 8 * a + size + 8] * tap_rows[8 * a + s : 8 * a + s + 1, column : column + LANES]
                        partial = term if partial is None else partial + term
                    if s:
                        partial = pltpu.roll(partial, size + 8 - s, 0)
                    total = total + partial[:size]
                swished[pl.ds(r0, size), column : column + LANES] = jax.nn.silu(total).astype(BF16)

    steps = rows // 64
    gate(0)
    comm(7)
    depthwise(0, 0, steps)
    gate(1)
    comm(8)
    depthwise(1, 0, steps)
    gate(2)
    comm(9)
    depthwise(2, 0, steps // 2)
    comm(10)
    depthwise(2, steps // 2, steps)

    @pl.loop(0, 16)
    def _(part):
        r0 = pl.multiple_of(part * 48, 48)
        flat_a = back_a.at[part // 4, lax.rem(part // 2, 2), pl.ds(lax.rem(part, 2) * 4, 4)]
        flat_b = back_b.at[part // 4, lax.rem(part // 2, 2), pl.ds(lax.rem(part, 2) * 4, 4)]
        back_w[pl.ds(r0, 48), :half] = flat_a[...].astype(F32).reshape(48, half).astype(BF16)
        back_w[pl.ds(r0, 48), half:] = flat_b[...].astype(F32).reshape(48, half).astype(BF16)

    error_cols[...] = jnp.zeros_like(error_cols)
    size = 2 * LANES
    vocab = 2 * quarter

    @pl.loop(0, rows // size)
    def _(part):
        r0 = pl.multiple_of(part * size, size)
        after = stem_out[pl.ds(r0 + HALO, size), :].astype(F32) + dot(swished[pl.ds(r0, size), :], back_w[...])
        second = normalised(after, gain_ref[0, 1:2, :])
        logits = jnp.concatenate(
            [dot(second, head_a[...].reshape(-1, quarter)), dot(second, head_b[...].reshape(-1, quarter))], axis=1
        )
        top = jnp.max(logits, axis=-1, keepdims=True)
        weight = jnp.exp(logits - top)
        posterior = weight * (1.0 / jnp.sum(weight, axis=-1, keepdims=True))
        token = lax.broadcasted_iota(jnp.int32, (LANES, vocab), 1).astype(F32)
        lane = lax.broadcasted_iota(jnp.int32, (LANES, LANES), 1)
        for k in range(2):
            here = lane == 2 * part + k
            target = jnp.sum(jnp.where(here, square[...], 0.0), axis=1, keepdims=True)
            onehot = jnp.where(token == target, 1.0, 0.0)
            differ = posterior[k * LANES : (k + 1) * LANES] - onehot
            norm = jnp.sqrt(jnp.sum(differ * differ, axis=-1, keepdims=True))
            error_cols[...] = jnp.where(here, norm, error_cols[...])

    block = lax.broadcasted_iota(jnp.int32, (blocks, LANES), 0)
    position = z * rows + block * LANES + lax.broadcasted_iota(jnp.int32, (blocks, LANES), 1)
    for b in range(blocks):
        square[b : b + 1, :] = mask_ref[0:1, b * LANES : (b + 1) * LANES].astype(F32)
    own = error_cols[...].T[:blocks] * jnp.where(position < length, 1.0, 0.0) * square[:blocks, :]
    seed_parts[x] = own
    sums = [
        pltpu.make_async_remote_copy(
            src_ref=seed_parts.at[x],
            dst_ref=seed_parts.at[x],
            send_sem=out_send.at[d],
            recv_sem=out_recv.at[d],
            device_id=(lax.rem(x + d, X), fsdp, z),
            device_id_type=MESH,
        )
        for d in range(1, X)
    ]
    for copy in sums:
        copy.start()
    for copy in sums:
        copy.wait()
    frame_error = (seed_parts[0] + seed_parts[1] + seed_parts[2] + seed_parts[3]) / 4.0
    for b in range(blocks):
        error_ref[0:1, b * LANES : (b + 1) * LANES] = frame_error[b : b + 1]
    seq_parts[z] = frame_error
    shares = [
        pltpu.make_async_remote_copy(
            src_ref=seq_parts.at[z],
            dst_ref=seq_parts.at[z],
            send_sem=out_send.at[X + d],
            recv_sem=out_recv.at[X + d],
            device_id=(x, fsdp, lax.rem(z + d, Z)),
            device_id_type=MESH,
        )
        for d in range(1, Z)
    ]
    for copy in shares:
        copy.start()
    for copy in shares:
        copy.wait()
    total = seq_parts[0]
    for k in range(1, Z):
        total = total + seq_parts[k]
    numerator = jnp.sum(jnp.sum(total, axis=1, keepdims=True), axis=0, keepdims=True)
    score_ref[...] = numerator / jnp.full((1, 1), length, jnp.int32).astype(F32)

    for copy in halo:
        copy.wait_send()
    for piece in pieces:
        piece.finish()


def body(mel, lengths, targets, mask, stem_weight, gate_weight, back_weight, depth_weight, head_weight, gain):
    rows = targets.shape[1]
    taps, channels = depth_weight.shape[1:]
    width = stem_weight.shape[2]
    wide = rows + 2 * HALO
    mels = mel.shape[2]
    mel_rows = 4 * HALO + mel.shape[1] + TAIL
    deep, thin = gate_weight.shape[1], back_weight.shape[1]
    vocab = head_weight.shape[2]
    vmem = pl.BlockSpec(memory_space=pltpu.VMEM)
    hbm = pl.BlockSpec(memory_space=pl.ANY)
    share = (Y, CORES, Z)
    blocks = rows // LANES
    flops = 2 * wide * width * (stem_weight.shape[1] + 2 * channels) + 2 * rows * width * (channels + vocab)
    error, score = pl.pallas_call(
        functools.partial(kernel, rows, taps),
        out_shape=(jax.ShapeDtypeStruct((1, rows), F32), jax.ShapeDtypeStruct((1, 1), F32)),
        in_specs=[pl.BlockSpec(memory_space=pltpu.SMEM)] + [vmem] * 4 + [hbm] * 5,
        out_specs=(vmem, vmem),
        scratch_shapes=[
            pltpu.VMEM((mel_rows, mels), BF16),
            pltpu.VMEM((mel_rows, mels), F32),
            pltpu.VMEM(stem_weight.shape[1:], BF16),
            pltpu.VMEM((GROUPS,) + share + (deep, GROUP), BF16),
            pltpu.VMEM((GROUPS,) + share + (deep, GROUP), BF16),
            pltpu.VMEM(share + (thin, width // 2), BF16),
            pltpu.VMEM(share + (thin, width // 2), BF16),
            pltpu.VMEM(share + (deep, vocab // 2), BF16),
            pltpu.VMEM(share + (deep, vocab // 2), BF16),
            pltpu.VMEM((channels, width), BF16),
            pltpu.VMEM((wide, width), BF16),
            pltpu.VMEM((wide, width), BF16),
            pltpu.VMEM((GROUP // LANES, wide, LANES), F32),
            pltpu.VMEM((rows, channels), BF16),
            pltpu.VMEM((32, channels), F32),
            pltpu.VMEM((LANES, LANES), F32),
            pltpu.VMEM((LANES, LANES), F32),
            pltpu.VMEM((X, blocks, LANES), F32),
            pltpu.VMEM((Z, blocks, LANES), F32),
            pltpu.SemaphoreType.DMA((10, 11)),
            pltpu.SemaphoreType.DMA((10, 11)),
            pltpu.SemaphoreType.DMA((12,)),
            pltpu.SemaphoreType.DMA((2,)),
            pltpu.SemaphoreType.DMA((2,)),
            pltpu.SemaphoreType.DMA((X + Z,)),
            pltpu.SemaphoreType.DMA((X + Z,)),
        ],
        compiler_params=pltpu.CompilerParams(
            collective_id=0, has_side_effects=True, vmem_limit_bytes=52 << 20
        ),
        cost_estimate=pl.CostEstimate(flops=flops, bytes_accessed=20 << 20, transcendentals=4 << 20),
        name="el2n_scores",
    )(lengths, targets, mask, gain, depth_weight, mel, stem_weight, gate_weight, back_weight, head_weight)
    return error, score.reshape(1)


def solution(mesh):
    in_specs = (
        P("fsdp", "seq", None),
        P("fsdp"),
        P("fsdp", "seq"),
        P("fsdp", "seq"),
        P("seed", None, None),
        P("seed", ("fsdp", "seq"), None),
        P("seed", ("fsdp", "seq"), None),
        P("seed", None, None),
        P("seed", ("fsdp", "seq"), None),
        P("seed", None, None),
    )
    out_specs = (P("fsdp", "seq"), P("fsdp"))
    return jax.shard_map(body, mesh=mesh, in_specs=in_specs, out_specs=out_specs, check_vma=False)
```

```python
import functools

import jax
import jax.numpy as jnp
from jax import lax
from jax.experimental import pallas as pl
from jax.experimental.pallas import tpu as pltpu
from jax.sharding import PartitionSpec as P

MESH = pl.DeviceIdType.MESH
F32 = jnp.float32
BF16 = jnp.bfloat16
HALO = 16
LANES = 128
GROUP = 256
GROUPS = 3
Y, CORES, Z, X = 4, 2, 8, 4
ORDER = (
    1, 0, 3, "misc", 4, "mel0", 1, 5, 0, 3, "mel1", 4, "stem0", 1, 2, 5, "stem1", 0, "stem2", 7, 3, 4,
    1, 2, 5, 9, 3, 0, 1, 6, 7, 2, 5, 0, 3, 1, 6, 8, 4, 9, 7, 1, "gate0", 4, 5, 3, "dw0a", 2, 8, 6, "dw0b",
    9, 7, 3, 2, "gate1", 5, 9, 8, "dw1a", 7, "dw1b", 9, 5, 6, "gate2", 7, "dw2a", 9, 8, 6, "dw2b", 7,
    "reloc", 9, 8, "fin",
)


class Piece:
    def __init__(self, place, own, dst, send, recv, local, y_first, flip):
        self.place, self.own, self.dst = place, own, dst
        self.send, self.recv, self.local = send, recv, local
        self.y_first, self.flip = y_first, flip
        self.used = 0
        self.copies = []
        self.pending = []
        self.round = 0

    def remote(self, src, dst, device):
        slot = self.used
        self.used += 1
        copy = pltpu.make_async_remote_copy(
            src_ref=src,
            dst_ref=dst,
            send_sem=self.send.at[slot],
            recv_sem=self.recv.at[slot],
            device_id=device,
            device_id_type=MESH,
        )
        copy.start()
        self.copies.append(copy)
        self.pending.append(copy)

    def at_z(self, by):
        x, y, c, z = self.place
        return (x, y * CORES + c, lax.rem(z + by + Z, Z))

    def at_y(self, by):
        x, y, c, z = self.place
        return (x, lax.rem(y + by + Y, Y) * CORES + c, z)

    def ring_step(self, step):
        x, y, c, z = self.place
        for sign in (1, -1):
            if step == 4 and sign == (-1 if self.flip else 1):
                continue
            block = self.dst.at[:, c, lax.rem(z - sign * (step - 1) + Z, Z)]
            self.remote(block, block, self.at_z(sign))

    def hop(self, by, to):
        x, y, c, z = self.place
        block = self.dst.at[y, c, lax.rem(z + by + Z, Z)]
        self.remote(self.own if by == 0 else block, block, self.at_z(to))

    def y_step(self):
        x, y, c, z = self.place
        block = self.dst.at[y, c, z] if self.y_first else self.dst.at[y, c]
        for by in (2, 1, 3):
            self.remote(self.own if self.y_first else block, block, self.at_y(by))

    def across(self):
        x, y, c, z = self.place
        block = self.dst.at[:, c]
        self.remote(block, block, (x, y * CORES + 1 - c, z))

    def arrived(self):
        for copy in self.pending:
            copy.wait_recv()
        self.pending = []

    def step(self):
        x, y, c, z = self.place
        now = self.round
        self.round += 1
        if now == 0:
            self.keep = pltpu.make_async_copy(self.own, self.dst.at[y, c, z], self.local)
            self.keep.start()
            if self.y_first:
                self.y_step()
            else:
                for by in (2, -2, 1, -1):
                    self.hop(0, by)
            return
        self.arrived()
        if now == 1:
            self.keep.wait()
        if self.y_first:
            if now <= 4:
                self.ring_step(now)
            elif now == 5:
                self.across()
        elif now == 1:
            self.hop(-1, 2)
            self.hop(-2, 2)
            self.hop(1, -2)
        elif now == 2:
            self.y_step()
        elif now == 3:
            self.across()

    def finish(self):
        for copy in self.copies:
            copy.wait_send()


def normalised(values, gain_row):
    row_mean = jnp.mean(values, axis=-1, keepdims=True)
    centred = values - row_mean
    row_var = jnp.mean(centred * centred, axis=-1, keepdims=True)
    return (centred * lax.rsqrt(row_var + 1e-05) * gain_row).astype(BF16)


def dot(left, right):
    return jnp.dot(left, right, preferred_element_type=F32)


def kernel(
    rows,
    taps,
    lengths_ref,
    targets_hbm,
    mask_hbm,
    gain_hbm,
    depth_hbm,
    mel_hbm,
    stem_hbm,
    gate_hbm,
    back_hbm,
    head_hbm,
    error_ref,
    score_ref,
    targets_ref,
    mask_ref,
    gain_ref,
    depth_ref,
    mel_bf,
    mel_f32,
    stem_w,
    gate_a,
    gate_b,
    back_a,
    back_b,
    head_a,
    head_b,
    back_w,
    stem_out,
    normed,
    gated,
    swished,
    tap_rows,
    square,
    error_cols,
    seed_parts,
    seq_parts,
    send_sem,
    recv_sem,
    local_sem,
    mel_send,
    mel_recv,
    out_send,
    out_recv,
):
    x = lax.axis_index("seed")
    fsdp = lax.axis_index("fsdp")
    y, c = fsdp // CORES, lax.rem(fsdp, CORES)
    z = lax.axis_index("seq")
    place = (x, y, c, z)
    wide = rows + 2 * HALO
    channels = GROUP * GROUPS

    barrier = pltpu.get_barrier_semaphore()
    peers = [(x, fsdp, lax.rem(z + d, Z)) for d in range(1, Z)]
    peers += [(x, lax.rem(y + d, Y) * CORES + c, z) for d in range(1, Y)]
    peers += [(lax.rem(x + d, X), fsdp, z) for d in range(1, X)]
    peers += [(x, y * CORES + 1 - c, z)]
    for peer in peers:
        pl.semaphore_signal(barrier, inc=1, device_id=peer, device_id_type=MESH)

    mel_rows = 4 * rows
    loads = [
        pltpu.make_async_copy(mel_hbm.at[0], mel_bf.at[:, pl.ds(LANES, mel_rows)], local_sem.at[10]),
        pltpu.make_async_copy(stem_hbm.at[0], stem_w, local_sem.at[11]),
        pltpu.make_async_copy(depth_hbm, depth_ref, local_sem.at[12]),
        pltpu.make_async_copy(targets_hbm, targets_ref, local_sem.at[13]),
        pltpu.make_async_copy(gain_hbm, gain_ref, local_sem.at[14]),
        pltpu.make_async_copy(mask_hbm, mask_ref, local_sem.at[15]),
    ]
    for load in loads:
        load.start()

    specs = []
    for group in range(GROUPS):
        specs.append((gate_hbm, GROUP * group, GROUP, gate_a.at[group], False))
        specs.append((gate_hbm, channels + GROUP * group, GROUP, gate_b.at[group], True))
    half = back_hbm.shape[2] // 2
    specs.append((back_hbm, 0, half, back_a, False))
    specs.append((back_hbm, half, half, back_b, True))
    quarter = head_hbm.shape[2] // 2
    specs.append((head_hbm, 0, quarter, head_a, False))
    specs.append((head_hbm, quarter, quarter, head_b, True))
    pieces = []
    for index, (source, start, width, dst, y_first) in enumerate(specs):
        own = source.at[0, :, pl.ds(start, width)]
        pieces.append(
            Piece(place, own, dst, send_sem.at[index], recv_sem.at[index], local_sem.at[index], y_first, index == 7)
        )
    pl.semaphore_wait(barrier, len(peers))
    halo = [
        pltpu.make_async_remote_copy(
            src_ref=mel_hbm.at[0, :, pl.ds(mel_rows - LANES, LANES)],
            dst_ref=mel_bf.at[:, pl.ds(0, LANES)],
            send_sem=mel_send.at[0],
            recv_sem=mel_recv.at[0],
            device_id=(x, fsdp, lax.rem(z + 1, Z)),
            device_id_type=MESH,
        ),
        pltpu.make_async_remote_copy(
            src_ref=mel_hbm.at[0, :, pl.ds(0, LANES)],
            dst_ref=mel_bf.at[:, pl.ds(LANES + mel_rows, LANES)],
            send_sem=mel_send.at[1],
            recv_sem=mel_recv.at[1],
            device_id=(x, fsdp, lax.rem(z + Z - 1, Z)),
            device_id_type=MESH,
        ),
    ]
    length = lengths_ref[0]
    blocks = rows // LANES

    def small():
        for load in loads:
            load.wait()
        tap_rows[...] = jnp.zeros_like(tap_rows)
        tap_rows[1 : 1 + taps, :] = depth_ref[0].astype(F32)
        square[...] = jnp.zeros_like(square)
        for b in range(blocks):
            square[b : b + 1, :] = targets_ref[0:1, b * LANES : (b + 1) * LANES].astype(F32)
        square[...] = square[...].T

    tiles = mel_rows // LANES + 2

    def upright(half):
        if half == 0:
            for copy in halo:
                copy.wait_recv()

        @pl.loop(half * (tiles // 2), (half + 1) * (tiles // 2))
        def _(part):
            r0 = pl.multiple_of(part * LANES, LANES)
            past = (z == Z - 1) & (part == tiles - 1)
            tile = jnp.where(past, 0.0, mel_bf[:, pl.ds(r0, LANES)].astype(F32))
            mel_f32[pl.ds(r0, LANES), :] = tile.T

    tall = wide // 3
    skip = LANES - 4 * HALO

    def stem(part):
        r0 = part * tall
        window = [mel_f32[pl.ds(skip + 4 * r0 + i, tall, stride=4), :] for i in range(8)]
        frames = jnp.concatenate(window, axis=1).astype(BF16)
        out = dot(frames, stem_w[...]).astype(BF16)
        stem_out[r0 : r0 + tall, :] = out
        normed[r0 : r0 + tall, :] = normalised(out.astype(F32), gain_ref[0, 0:1, :])

    def gate(group):
        @pl.loop(0, 3)
        def _(part):
            r0 = pl.multiple_of(part * tall, 16)
            left = normed[pl.ds(r0, tall), :]
            value = dot(left, gate_a[group].reshape(-1, GROUP))
            control = dot(left, gate_b[group].reshape(-1, GROUP))
            position = z * rows - HALO + r0 + lax.broadcasted_iota(jnp.int32, (tall, 1), 0)
            live = jnp.where((position >= 0) & (position < length), 1.0, 0.0).astype(F32)
            result = (value * jax.nn.sigmoid(control) * live).astype(BF16).astype(F32)
            for k in range(GROUP // LANES):
                gated[k, pl.ds(r0, tall), :] = result[:, k * LANES : (k + 1) * LANES]

    def depthwise(group, first, last):
        size = 64

        @pl.loop(first, last)
        def _(part):
            r0 = pl.multiple_of(part * size, size)
            for k in range(GROUP // LANES):
                column = group * GROUP + k * LANES
                around = gated[k, pl.ds(r0, size + 32), :]
                total = jnp.zeros((size, LANES), F32)
                for s in range(8):
                    partial = None
                    for a in range(4):
                        if a == 0 and s == 0:
                            continue
                        term = around[8 * a : 8 * a + size + 8] * tap_rows[8 * a + s : 8 * a + s + 1, column : column + LANES]
                        partial = term if partial is None else partial + term
                    if s:
                        partial = pltpu.roll(partial, size + 8 - s, 0)
                    total = total + partial[:size]
                swished[pl.ds(r0, size), column : column + LANES] = jax.nn.silu(total).astype(BF16)

    def contiguous():
        error_cols[...] = jnp.zeros_like(error_cols)

        @pl.loop(0, 16)
        def _(part):
            r0 = pl.multiple_of(part * 48, 48)
            flat_a = back_a.at[part // 4, lax.rem(part // 2, 2), pl.ds(lax.rem(part, 2) * 4, 4)]
            flat_b = back_b.at[part // 4, lax.rem(part // 2, 2), pl.ds(lax.rem(part, 2) * 4, 4)]
            back_w[pl.ds(r0, 48), :half] = flat_a[...].astype(F32).reshape(48, half).astype(BF16)
            back_w[pl.ds(r0, 48), half:] = flat_b[...].astype(F32).reshape(48, half).astype(BF16)

    def scores():
        size = 2 * LANES
        vocab = 2 * quarter

        @pl.loop(0, rows // size)
        def _(part):
            r0 = pl.multiple_of(part * size, size)
            after = stem_out[pl.ds(r0 + HALO, size), :].astype(F32) + dot(swished[pl.ds(r0, size), :], back_w[...])
            second = normalised(after, gain_ref[0, 1:2, :])
            logits = jnp.concatenate(
                [dot(second, head_a[...].reshape(-1, quarter)), dot(second, head_b[...].reshape(-1, quarter))], axis=1
            )
            top = jnp.max(logits, axis=-1, keepdims=True)
            weight = jnp.exp(logits - top)
            posterior = weight * (1.0 / jnp.sum(weight, axis=-1, keepdims=True))
            token = lax.broadcasted_iota(jnp.int32, (LANES, vocab), 1).astype(F32)
            lane = lax.broadcasted_iota(jnp.int32, (LANES, LANES), 1)
            for k in range(2):
                here = lane == 2 * part + k
                target = jnp.sum(jnp.where(here, square[...], 0.0), axis=1, keepdims=True)
                onehot = jnp.where(token == target, 1.0, 0.0)
                differ = posterior[k * LANES : (k + 1) * LANES] - onehot
                norm = jnp.sqrt(jnp.sum(differ * differ, axis=-1, keepdims=True))
                error_cols[...] = jnp.where(here, norm, error_cols[...])

    steps = rows // 64 // 2
    work = {"misc": small, "reloc": contiguous, "fin": scores}
    for k in range(2):
        work["mel%d" % k] = functools.partial(upright, k)
    for k in range(3):
        work["stem%d" % k] = functools.partial(stem, k)
    for k in range(GROUPS):
        work["gate%d" % k] = functools.partial(gate, k)
        work["dw%da" % k] = functools.partial(depthwise, k, 0, steps)
        work["dw%db" % k] = functools.partial(depthwise, k, steps, 2 * steps)
    sent_halo = False
    for token in ORDER:
        if not isinstance(token, int):
            if not sent_halo:
                for copy in halo:
                    copy.start()
                sent_halo = True
            work[token]()
        else:
            pieces[token].step()

    block = lax.broadcasted_iota(jnp.int32, (blocks, LANES), 0)
    position = z * rows + block * LANES + lax.broadcasted_iota(jnp.int32, (blocks, LANES), 1)
    for b in range(blocks):
        square[b : b + 1, :] = mask_ref[0:1, b * LANES : (b + 1) * LANES].astype(F32)
    own = error_cols[...].T[:blocks] * jnp.where(position < length, 1.0, 0.0) * square[:blocks, :]
    seed_parts[x] = own
    sums = [
        pltpu.make_async_remote_copy(
            src_ref=seed_parts.at[x],
            dst_ref=seed_parts.at[x],
            send_sem=out_send.at[d],
            recv_sem=out_recv.at[d],
            device_id=(lax.rem(x + d, X), fsdp, z),
            device_id_type=MESH,
        )
        for d in range(1, X)
    ]
    for copy in sums:
        copy.start()
    for copy in sums:
        copy.wait()
    frame_error = (seed_parts[0] + seed_parts[1] + seed_parts[2] + seed_parts[3]) / 4.0
    for b in range(blocks):
        error_ref[0:1, b * LANES : (b + 1) * LANES] = frame_error[b : b + 1]
    seq_parts[z] = frame_error
    shares = [
        pltpu.make_async_remote_copy(
            src_ref=seq_parts.at[z],
            dst_ref=seq_parts.at[z],
            send_sem=out_send.at[X + d],
            recv_sem=out_recv.at[X + d],
            device_id=(x, fsdp, lax.rem(z + d, Z)),
            device_id_type=MESH,
        )
        for d in range(1, Z)
    ]
    for copy in shares:
        copy.start()
    for copy in shares:
        copy.wait()
    total = seq_parts[0]
    for k in range(1, Z):
        total = total + seq_parts[k]
    numerator = jnp.sum(jnp.sum(total, axis=1, keepdims=True), axis=0, keepdims=True)
    score_ref[...] = numerator / jnp.full((1, 1), length, jnp.int32).astype(F32)

    for copy in halo:
        copy.wait_send()
    for piece in pieces:
        piece.finish()


def body(mel, lengths, targets, mask, stem_weight, gate_weight, back_weight, depth_weight, head_weight, gain):
    rows = targets.shape[1]
    taps, channels = depth_weight.shape[1:]
    width = stem_weight.shape[2]
    wide = rows + 2 * HALO
    mels = mel.shape[2]
    mel_rows = mel.shape[1] + 2 * LANES
    deep, thin = gate_weight.shape[1], back_weight.shape[1]
    vocab = head_weight.shape[2]
    vmem = pl.BlockSpec(memory_space=pltpu.VMEM)
    hbm = pl.BlockSpec(memory_space=pltpu.HBM)
    share = (Y, CORES, Z)
    blocks = rows // LANES
    flops = 2 * wide * width * (stem_weight.shape[1] + 2 * channels) + 2 * rows * width * (channels + vocab)
    error, score = pl.pallas_call(
        functools.partial(kernel, rows, taps),
        out_shape=(jax.ShapeDtypeStruct((1, rows), F32), jax.ShapeDtypeStruct((1, 1), F32)),
        in_specs=[pl.BlockSpec(memory_space=pltpu.SMEM)] + [hbm] * 9,
        out_specs=(vmem, vmem),
        scratch_shapes=[
            pltpu.VMEM(targets.shape, jnp.int32),
            pltpu.VMEM(mask.shape, jnp.int32),
            pltpu.VMEM(gain.shape, F32),
            pltpu.VMEM(depth_weight.shape, BF16),
            pltpu.VMEM((mels, mel_rows), BF16),
            pltpu.VMEM((mel_rows, mels), F32),
            pltpu.VMEM(stem_weight.shape[1:], BF16),
            pltpu.VMEM((GROUPS,) + share + (deep, GROUP), BF16),
            pltpu.VMEM((GROUPS,) + share + (deep, GROUP), BF16),
            pltpu.VMEM(share + (thin, width // 2), BF16),
            pltpu.VMEM(share + (thin, width // 2), BF16),
            pltpu.VMEM(share + (deep, vocab // 2), BF16),
            pltpu.VMEM(share + (deep, vocab // 2), BF16),
            pltpu.VMEM((channels, width), BF16),
            pltpu.VMEM((wide, width), BF16),
            pltpu.VMEM((wide, width), BF16),
            pltpu.VMEM((GROUP // LANES, wide, LANES), F32),
            pltpu.VMEM((rows, channels), BF16),
            pltpu.VMEM((32, channels), F32),
            pltpu.VMEM((LANES, LANES), F32),
            pltpu.VMEM((LANES, LANES), F32),
            pltpu.VMEM((X, blocks, LANES), F32),
            pltpu.VMEM((Z, blocks, LANES), F32),
            pltpu.SemaphoreType.DMA((10, 11)),
            pltpu.SemaphoreType.DMA((10, 11)),
            pltpu.SemaphoreType.DMA((16,)),
            pltpu.SemaphoreType.DMA((2,)),
            pltpu.SemaphoreType.DMA((2,)),
            pltpu.SemaphoreType.DMA((X + Z,)),
            pltpu.SemaphoreType.DMA((X + Z,)),
        ],
        compiler_params=pltpu.CompilerParams(
            collective_id=0, has_side_effects=True, vmem_limit_bytes=64 << 20
        ),
        cost_estimate=pl.CostEstimate(flops=flops, bytes_accessed=20 << 20, transcendentals=4 << 20),
        name="el2n_scores",
    )(lengths, targets, mask, gain, depth_weight, jnp.swapaxes(mel, 1, 2), stem_weight, gate_weight, back_weight, head_weight)
    return error, score.reshape(1)


def solution(mesh):
    in_specs = (
        P("fsdp", "seq", None),
        P("fsdp"),
        P("fsdp", "seq"),
        P("fsdp", "seq"),
        P("seed", None, None),
        P("seed", ("fsdp", "seq"), None),
        P("seed", ("fsdp", "seq"), None),
        P("seed", None, None),
        P("seed", ("fsdp", "seq"), None),
        P("seed", None, None),
    )
    out_specs = (P("fsdp", "seq"), P("fsdp"))
    return jax.shard_map(body, mesh=mesh, in_specs=in_specs, out_specs=out_specs, check_vma=False)
```

```python
import functools

import jax
import jax.numpy as jnp
from jax import lax
from jax.experimental import pallas as pl
from jax.experimental.pallas import tpu as pltpu
from jax.sharding import PartitionSpec as P

MESH = pl.DeviceIdType.MESH
F32 = jnp.float32
BF16 = jnp.bfloat16
HALO = 16
LANES = 128
GROUP = 256
GROUPS = 3
Y, CORES, Z, X = 4, 2, 8, 4
ORDER = (
    1, 0, 3, "misc", 4, "mel0", 1, 5, 0, 3, "mel1", 4, "stem0", 1, 2, 5, "stem1", 0, "stem2", 7, 3, 4,
    1, 2, 5, 9, 3, 0, 1, 6, 7, 2, 5, 0, 3, 1, 6, 8, 4, 9, 7, 1, "gate0", 4, 5, 3, "dw0a", 2, 8, 6, "dw0b",
    9, 7, 3, 2, "gate1", 5, 9, 8, "dw1a", 7, "dw1b", 9, 5, 6, "gate2", 7, "dw2a", 9, 8, 6, "dw2b", 7,
    "reloc", 9, 8, "finA", "finB",
)


class Piece:
    def __init__(self, place, own, dst, send, recv, local, y_first, flip):
        self.place, self.own, self.dst = place, own, dst
        self.send, self.recv, self.local = send, recv, local
        self.y_first, self.flip = y_first, flip
        self.used = 0
        self.copies = []
        self.pending = []
        self.round = 0

    def remote(self, src, dst, device):
        slot = self.used
        self.used += 1
        copy = pltpu.make_async_remote_copy(
            src_ref=src,
            dst_ref=dst,
            send_sem=self.send.at[slot],
            recv_sem=self.recv.at[slot],
            device_id=device,
            device_id_type=MESH,
        )
        copy.start()
        self.copies.append(copy)
        self.pending.append(copy)

    def at_z(self, by):
        x, y, c, z = self.place
        return (x, y * CORES + c, lax.rem(z + by + Z, Z))

    def at_y(self, by):
        x, y, c, z = self.place
        return (x, lax.rem(y + by + Y, Y) * CORES + c, z)

    def ring_step(self, step):
        x, y, c, z = self.place
        for sign in (1, -1):
            if step == 4 and sign == (-1 if self.flip else 1):
                continue
            block = self.dst.at[:, c, lax.rem(z - sign * (step - 1) + Z, Z)]
            self.remote(block, block, self.at_z(sign))

    def hop(self, by, to):
        x, y, c, z = self.place
        block = self.dst.at[y, c, lax.rem(z + by + Z, Z)]
        self.remote(self.own if by == 0 else block, block, self.at_z(to))

    def y_step(self):
        x, y, c, z = self.place
        block = self.dst.at[y, c, z] if self.y_first else self.dst.at[y, c]
        for by in (2, 1, 3):
            self.remote(self.own if self.y_first else block, block, self.at_y(by))

    def across(self):
        x, y, c, z = self.place
        block = self.dst.at[:, c]
        self.remote(block, block, (x, y * CORES + 1 - c, z))

    def arrived(self):
        for copy in self.pending:
            copy.wait_recv()
        self.pending = []

    def step(self):
        x, y, c, z = self.place
        now = self.round
        self.round += 1
        if now == 0:
            self.keep = pltpu.make_async_copy(self.own, self.dst.at[y, c, z], self.local)
            self.keep.start()
            if self.y_first:
                self.y_step()
            else:
                for by in (2, -2, 1, -1):
                    self.hop(0, by)
            return
        self.arrived()
        if now == 1:
            self.keep.wait()
        if self.y_first:
            if now <= 4:
                self.ring_step(now)
            elif now == 5:
                self.across()
        elif now == 1:
            self.hop(-1, 2)
            self.hop(-2, 2)
            self.hop(1, -2)
        elif now == 2:
            self.y_step()
        elif now == 3:
            self.across()

    def finish(self):
        for copy in self.copies:
            copy.wait_send()


def normalised(values, gain_row):
    row_mean = jnp.mean(values, axis=-1, keepdims=True)
    centred = values - row_mean
    row_var = jnp.mean(centred * centred, axis=-1, keepdims=True)
    return (centred * lax.rsqrt(row_var + 1e-05) * gain_row).astype(BF16)


def dot(left, right):
    return jnp.dot(left, right, preferred_element_type=F32)


def kernel(
    rows,
    taps,
    lengths_ref,
    targets_hbm,
    mask_hbm,
    gain_hbm,
    depth_hbm,
    mel_hbm,
    stem_hbm,
    gate_hbm,
    back_hbm,
    head_hbm,
    error_ref,
    score_ref,
    targets_ref,
    mask_ref,
    gain_ref,
    depth_ref,
    mel_bf,
    mel_f32,
    stem_w,
    gate_a,
    gate_b,
    back_a,
    back_b,
    head_a,
    head_b,
    back_w,
    stem_out,
    normed,
    gated,
    swished,
    tap_rows,
    square,
    error_cols,
    seed_parts,
    seq_parts,
    send_sem,
    recv_sem,
    local_sem,
    mel_send,
    mel_recv,
    out_send,
    out_recv,
):
    x = lax.axis_index("seed")
    fsdp = lax.axis_index("fsdp")
    y, c = fsdp // CORES, lax.rem(fsdp, CORES)
    z = lax.axis_index("seq")
    place = (x, y, c, z)
    wide = rows + 2 * HALO
    channels = GROUP * GROUPS

    barrier = pltpu.get_barrier_semaphore()
    peers = [(lax.rem(x + d, X), fsdp, lax.rem(z + e, Z)) for d in range(X) for e in range(Z) if d or e]
    peers += [(x, lax.rem(y + d, Y) * CORES + c, z) for d in range(1, Y)]
    peers += [(x, y * CORES + 1 - c, z)]
    for peer in peers:
        pl.semaphore_signal(barrier, inc=1, device_id=peer, device_id_type=MESH)

    mel_rows = 4 * rows
    loads = [
        pltpu.make_async_copy(mel_hbm.at[0], mel_bf.at[:, pl.ds(LANES, mel_rows)], local_sem.at[10]),
        pltpu.make_async_copy(stem_hbm.at[0], stem_w, local_sem.at[11]),
        pltpu.make_async_copy(depth_hbm, depth_ref, local_sem.at[12]),
        pltpu.make_async_copy(targets_hbm, targets_ref, local_sem.at[13]),
        pltpu.make_async_copy(gain_hbm, gain_ref, local_sem.at[14]),
        pltpu.make_async_copy(mask_hbm, mask_ref, local_sem.at[15]),
    ]
    for load in loads:
        load.start()

    specs = []
    for group in range(GROUPS):
        specs.append((gate_hbm, GROUP * group, GROUP, gate_a.at[group], False))
        specs.append((gate_hbm, channels + GROUP * group, GROUP, gate_b.at[group], True))
    half = back_hbm.shape[2] // 2
    specs.append((back_hbm, 0, half, back_a, False))
    specs.append((back_hbm, half, half, back_b, True))
    quarter = head_hbm.shape[2] // 2
    specs.append((head_hbm, 0, quarter, head_a, False))
    specs.append((head_hbm, quarter, quarter, head_b, True))
    pieces = []
    for index, (source, start, width, dst, y_first) in enumerate(specs):
        own = source.at[0, :, pl.ds(start, width)]
        pieces.append(
            Piece(place, own, dst, send_sem.at[index], recv_sem.at[index], local_sem.at[index], y_first, index == 7)
        )
    pl.semaphore_wait(barrier, len(peers))
    halo = [
        pltpu.make_async_remote_copy(
            src_ref=mel_hbm.at[0, :, pl.ds(mel_rows - LANES, LANES)],
            dst_ref=mel_bf.at[:, pl.ds(0, LANES)],
            send_sem=mel_send.at[0],
            recv_sem=mel_recv.at[0],
            device_id=(x, fsdp, lax.rem(z + 1, Z)),
            device_id_type=MESH,
        ),
        pltpu.make_async_remote_copy(
            src_ref=mel_hbm.at[0, :, pl.ds(0, LANES)],
            dst_ref=mel_bf.at[:, pl.ds(LANES + mel_rows, LANES)],
            send_sem=mel_send.at[1],
            recv_sem=mel_recv.at[1],
            device_id=(x, fsdp, lax.rem(z + Z - 1, Z)),
            device_id_type=MESH,
        ),
    ]
    length = lengths_ref[0]
    blocks = rows // LANES

    def small():
        for load in loads:
            load.wait()
        tap_rows[...] = jnp.zeros_like(tap_rows)
        tap_rows[1 : 1 + taps, :] = depth_ref[0].astype(F32)
        square[...] = jnp.zeros_like(square)
        for b in range(blocks):
            square[b : b + 1, :] = targets_ref[0:1, b * LANES : (b + 1) * LANES].astype(F32)
        square[...] = square[...].T

    tiles = mel_rows // LANES + 2

    def upright(half):
        if half == 0:
            for copy in halo:
                copy.wait_recv()

        @pl.loop(half * (tiles // 2), (half + 1) * (tiles // 2))
        def _(part):
            r0 = pl.multiple_of(part * LANES, LANES)
            past = (z == Z - 1) & (part == tiles - 1)
            tile = jnp.where(past, 0.0, mel_bf[:, pl.ds(r0, LANES)].astype(F32))
            mel_f32[pl.ds(r0, LANES), :] = tile.T

    tall = wide // 3
    skip = LANES - 4 * HALO

    def stem(part):
        r0 = part * tall
        window = [mel_f32[pl.ds(skip + 4 * r0 + i, tall, stride=4), :] for i in range(8)]
        frames = jnp.concatenate(window, axis=1).astype(BF16)
        out = dot(frames, stem_w[...]).astype(BF16)
        stem_out[r0 : r0 + tall, :] = out
        normed[r0 : r0 + tall, :] = normalised(out.astype(F32), gain_ref[0, 0:1, :])

    def gate(group):
        for part in range(3):
            r0 = part * tall
            left = normed[pl.ds(r0, tall), :]
            value = dot(left, gate_a[group].reshape(-1, GROUP))
            control = dot(left, gate_b[group].reshape(-1, GROUP))
            position = z * rows - HALO + r0 + lax.broadcasted_iota(jnp.int32, (tall, 1), 0)
            live = jnp.where((position >= 0) & (position < length), 1.0, 0.0).astype(F32)
            result = (value * jax.nn.sigmoid(control) * live).astype(BF16).astype(F32)
            for k in range(GROUP // LANES):
                gated[k, pl.ds(r0, tall), :] = result[:, k * LANES : (k + 1) * LANES]

    def depthwise(group, first, last):
        size = 128

        @pl.loop(first, last)
        def _(part):
            r0 = pl.multiple_of(part * size, size)
            for k in range(GROUP // LANES):
                column = group * GROUP + k * LANES
                around = gated[k, pl.ds(r0, size + 32), :]
                total = jnp.zeros((size, LANES), F32)
                for s in range(8):
                    partial = None
                    for a in range(4):
                        if a == 0 and s == 0:
                            continue
                        term = around[8 * a : 8 * a + size + 8] * tap_rows[8 * a + s : 8 * a + s + 1, column : column + LANES]
                        partial = term if partial is None else partial + term
                    if s:
                        partial = pltpu.roll(partial, size + 8 - s, 0)
                    total = total + partial[:size]
                swished[pl.ds(r0, size), column : column + LANES] = jax.nn.silu(total).astype(BF16)

    def contiguous():
        error_cols[...] = jnp.zeros_like(error_cols)

        @pl.loop(0, 16)
        def _(part):
            r0 = pl.multiple_of(part * 48, 48)
            flat_a = back_a.at[part // 4, lax.rem(part // 2, 2), pl.ds(lax.rem(part, 2) * 4, 4)]
            flat_b = back_b.at[part // 4, lax.rem(part // 2, 2), pl.ds(lax.rem(part, 2) * 4, 4)]
            back_w[pl.ds(r0, 48), :half] = flat_a[...].astype(F32).reshape(48, half).astype(BF16)
            back_w[pl.ds(r0, 48), half:] = flat_b[...].astype(F32).reshape(48, half).astype(BF16)

    size = 4 * LANES

    def project():
        @pl.loop(0, rows // size)
        def _(part):
            r0 = pl.multiple_of(part * size, size)
            product = dot(swished[pl.ds(r0, size), :], back_w[...])
            after = stem_out[pl.ds(r0 + HALO, size), :].astype(F32) + product
            normed[pl.ds(r0, size), :] = normalised(after, gain_ref[0, 1:2, :])

    def scores():
        @pl.loop(0, rows // size)
        def _(part):
            r0 = pl.multiple_of(part * size, size)
            second = normed[pl.ds(r0, size), :]
            logits = jnp.concatenate(
                [dot(second, head_a[...].reshape(-1, quarter)), dot(second, head_b[...].reshape(-1, quarter))], axis=1
            )
            top = jnp.max(logits, axis=-1, keepdims=True)
            weight = jnp.exp(logits - top)
            posterior = weight * (1.0 / jnp.sum(weight, axis=-1, keepdims=True))
            token = lax.broadcasted_iota(jnp.int32, (LANES, 2 * quarter), 1).astype(F32)
            lane = lax.broadcasted_iota(jnp.int32, (LANES, LANES), 1)
            for k in range(size // LANES):
                here = lane == size // LANES * part + k
                target = jnp.sum(jnp.where(here, square[...], 0.0), axis=1, keepdims=True)
                onehot = jnp.where(token == target, 1.0, 0.0)
                differ = posterior[k * LANES : (k + 1) * LANES] - onehot
                norm = jnp.sqrt(jnp.sum(differ * differ, axis=-1, keepdims=True))
                error_cols[...] = jnp.where(here, norm, error_cols[...])

    steps = rows // 128 // 2
    work = {"misc": small, "reloc": contiguous, "finA": project, "finB": scores}
    for k in range(2):
        work["mel%d" % k] = functools.partial(upright, k)
    for k in range(3):
        work["stem%d" % k] = functools.partial(stem, k)
    for k in range(GROUPS):
        work["gate%d" % k] = functools.partial(gate, k)
        work["dw%da" % k] = functools.partial(depthwise, k, 0, steps)
        work["dw%db" % k] = functools.partial(depthwise, k, steps, 2 * steps)
    sent_halo = False
    for token in ORDER:
        if not isinstance(token, int):
            if not sent_halo:
                for copy in halo:
                    copy.start()
                sent_halo = True
            work[token]()
        else:
            pieces[token].step()

    block = lax.broadcasted_iota(jnp.int32, (blocks, LANES), 0)
    position = z * rows + block * LANES + lax.broadcasted_iota(jnp.int32, (blocks, LANES), 1)
    for b in range(blocks):
        square[b : b + 1, :] = mask_ref[0:1, b * LANES : (b + 1) * LANES].astype(F32)
    own = error_cols[...].T[:blocks] * jnp.where(position < length, 1.0, 0.0) * square[:blocks, :]
    seed_parts[x] = own
    seq_parts[x, z] = jnp.sum(own, axis=0, keepdims=True)
    copies = []
    for d in range(1, X):
        copies.append((seed_parts.at[x], (lax.rem(x + d, X), fsdp, z)))
    for e in (4, 3, 5, 2, 6, 1, 7, 0):
        for d in (2, 1, 3, 0):
            if d or e:
                copies.append((seq_parts.at[x, z], (lax.rem(x + d, X), fsdp, lax.rem(z + e, Z))))
    copies = [
        pltpu.make_async_remote_copy(
            src_ref=ref,
            dst_ref=ref,
            send_sem=out_send.at[k],
            recv_sem=out_recv.at[k],
            device_id=device,
            device_id_type=MESH,
        )
        for k, (ref, device) in enumerate(copies)
    ]
    for copy in copies:
        copy.start()
    for copy in copies[: X - 1]:
        copy.wait()
    frame_error = (seed_parts[0] + seed_parts[1] + seed_parts[2] + seed_parts[3]) / 4.0
    for b in range(blocks):
        error_ref[0:1, b * LANES : (b + 1) * LANES] = frame_error[b : b + 1]
    for copy in copies[X - 1 :]:
        copy.wait()
    total = jnp.sum(seq_parts[...].reshape(X * Z, LANES), axis=0, keepdims=True) / 4.0
    numerator = jnp.sum(total, axis=1, keepdims=True)
    score_ref[...] = numerator / jnp.full((1, 1), length, jnp.int32).astype(F32)

    for copy in halo:
        copy.wait_send()
    for piece in pieces:
        piece.finish()


def body(mel, lengths, targets, mask, stem_weight, gate_weight, back_weight, depth_weight, head_weight, gain):
    rows = targets.shape[1]
    taps, channels = depth_weight.shape[1:]
    width = stem_weight.shape[2]
    wide = rows + 2 * HALO
    mels = mel.shape[2]
    mel_rows = mel.shape[1] + 2 * LANES
    deep, thin = gate_weight.shape[1], back_weight.shape[1]
    vocab = head_weight.shape[2]
    vmem = pl.BlockSpec(memory_space=pltpu.VMEM)
    hbm = pl.BlockSpec(memory_space=pltpu.HBM)
    share = (Y, CORES, Z)
    blocks = rows // LANES
    flops = 2 * wide * width * (stem_weight.shape[1] + 2 * channels) + 2 * rows * width * (channels + vocab)
    error, score = pl.pallas_call(
        functools.partial(kernel, rows, taps),
        out_shape=(jax.ShapeDtypeStruct((1, rows), F32), jax.ShapeDtypeStruct((1, 1), F32)),
        in_specs=[pl.BlockSpec(memory_space=pltpu.SMEM)] + [hbm] * 9,
        out_specs=(vmem, vmem),
        scratch_shapes=[
            pltpu.VMEM(targets.shape, jnp.int32),
            pltpu.VMEM(mask.shape, jnp.int32),
            pltpu.VMEM(gain.shape, F32),
            pltpu.VMEM(depth_weight.shape, BF16),
            pltpu.VMEM((mels, mel_rows), BF16),
            pltpu.VMEM((mel_rows, mels), F32),
            pltpu.VMEM(stem_weight.shape[1:], BF16),
            pltpu.VMEM((GROUPS,) + share + (deep, GROUP), BF16),
            pltpu.VMEM((GROUPS,) + share + (deep, GROUP), BF16),
            pltpu.VMEM(share + (thin, width // 2), BF16),
            pltpu.VMEM(share + (thin, width // 2), BF16),
            pltpu.VMEM(share + (deep, vocab // 2), BF16),
            pltpu.VMEM(share + (deep, vocab // 2), BF16),
            pltpu.VMEM((channels, width), BF16),
            pltpu.VMEM((wide, width), BF16),
            pltpu.VMEM((wide, width), BF16),
            pltpu.VMEM((GROUP // LANES, wide, LANES), F32),
            pltpu.VMEM((rows, channels), BF16),
            pltpu.VMEM((32, channels), F32),
            pltpu.VMEM((LANES, LANES), F32),
            pltpu.VMEM((LANES, LANES), F32),
            pltpu.VMEM((X, blocks, LANES), F32),
            pltpu.VMEM((X, Z, 1, LANES), F32),
            pltpu.SemaphoreType.DMA((10, 11)),
            pltpu.SemaphoreType.DMA((10, 11)),
            pltpu.SemaphoreType.DMA((16,)),
            pltpu.SemaphoreType.DMA((2,)),
            pltpu.SemaphoreType.DMA((2,)),
            pltpu.SemaphoreType.DMA((X - 1 + X * Z - 1,)),
            pltpu.SemaphoreType.DMA((X - 1 + X * Z - 1,)),
        ],
        compiler_params=pltpu.CompilerParams(
            collective_id=0, has_side_effects=True, vmem_limit_bytes=64 << 20
        ),
        cost_estimate=pl.CostEstimate(flops=flops, bytes_accessed=20 << 20, transcendentals=4 << 20),
        name="el2n_scores",
    )(lengths, targets, mask, gain, depth_weight, jnp.swapaxes(mel, 1, 2), stem_weight, gate_weight, back_weight, head_weight)
    return error, score.reshape(1)


def solution(mesh):
    in_specs = (
        P("fsdp", "seq", None),
        P("fsdp"),
        P("fsdp", "seq"),
        P("fsdp", "seq"),
        P("seed", None, None),
        P("seed", ("fsdp", "seq"), None),
        P("seed", ("fsdp", "seq"), None),
        P("seed", None, None),
        P("seed", ("fsdp", "seq"), None),
        P("seed", None, None),
    )
    out_specs = (P("fsdp", "seq"), P("fsdp"))
    return jax.shard_map(body, mesh=mesh, in_specs=in_specs, out_specs=out_specs, check_vma=False)
```

```python
import functools

import jax
import jax.numpy as jnp
from jax import lax
from jax.experimental import pallas as pl
from jax.experimental.pallas import tpu as pltpu
from jax.sharding import PartitionSpec as P

MESH = pl.DeviceIdType.MESH
F32 = jnp.float32
BF16 = jnp.bfloat16
HALO = 16
LANES = 128
GROUP = 256
GROUPS = 3
Y, CORES, Z, X = 4, 2, 8, 4
ORDER = (
    1, 2, 0, "misc", 4, "mel0", 1, 2, 3, "mel1", 5, 0, 4, "stem0", 1, 3, "stem1", 2, "stem2", 5, 7, 6,
    0, 4, 9, 1, 3, 5, 6, 2, 1, 7, 3, 8, 5, 2, 1, 6, 0, 7, 3, 1, 8, 0, "gate0", 5, 9, 4, "dw0a", 3, 7,
    8, "dw0b", 5, 4, 9, 3, "gate1", 5, 7, 6, "dw1a", 9, "dw1b", "gate2", 7, 8, 6, 9, "dw2a", "dw2b", 7,
    "reloc", 9, "finA", 8, 9, "finB",
)


class Piece:
    def __init__(self, place, own, dst, send, recv, local, y_first, flip):
        self.place, self.own, self.dst = place, own, dst
        self.send, self.recv, self.local = send, recv, local
        self.y_first, self.flip = y_first, flip
        self.used = 0
        self.copies = []
        self.pending = []
        self.round = 0

    def remote(self, src, dst, device):
        slot = self.used
        self.used += 1
        copy = pltpu.make_async_remote_copy(
            src_ref=src,
            dst_ref=dst,
            send_sem=self.send.at[slot],
            recv_sem=self.recv.at[slot],
            device_id=device,
            device_id_type=MESH,
        )
        copy.start()
        self.copies.append(copy)
        self.pending.append(copy)

    def at_z(self, by):
        x, y, c, z = self.place
        return (x, y * CORES + c, lax.rem(z + by + Z, Z))

    def at_y(self, by):
        x, y, c, z = self.place
        return (x, lax.rem(y + by + Y, Y) * CORES + c, z)

    def ring_step(self, step):
        x, y, c, z = self.place
        for sign in (1, -1):
            if step == 4 and sign == (-1 if self.flip else 1):
                continue
            block = self.dst.at[:, c, lax.rem(z - sign * (step - 1) + Z, Z)]
            self.remote(block, block, self.at_z(sign))

    def hop(self, by, to):
        x, y, c, z = self.place
        block = self.dst.at[y, c, lax.rem(z + by + Z, Z)]
        self.remote(self.own if by == 0 else block, block, self.at_z(to))

    def y_step(self):
        x, y, c, z = self.place
        block = self.dst.at[y, c, z] if self.y_first else self.dst.at[y, c]
        for by in (2, 1, 3):
            self.remote(self.own if self.y_first else block, block, self.at_y(by))

    def across(self):
        x, y, c, z = self.place
        block = self.dst.at[:, c]
        self.remote(block, block, (x, y * CORES + 1 - c, z))

    def arrived(self):
        for copy in self.pending:
            copy.wait_recv()
        self.pending = []

    def step(self):
        x, y, c, z = self.place
        now = self.round
        self.round += 1
        if now == 0:
            self.keep = pltpu.make_async_copy(self.own, self.dst.at[y, c, z], self.local)
            self.keep.start()
            if self.y_first:
                self.y_step()
            else:
                for by in (2, -2, 1, -1):
                    self.hop(0, by)
            return
        self.arrived()
        if now == 1:
            self.keep.wait()
        if self.y_first:
            if now <= 4:
                self.ring_step(now)
            elif now == 5:
                self.across()
        elif now == 1:
            self.hop(-1, 2)
            self.hop(-2, 2)
            self.hop(1, -2)
        elif now == 2:
            self.y_step()
        elif now == 3:
            self.across()

    def finish(self):
        for copy in self.copies:
            copy.wait_send()


def normalised(values, gain_row):
    row_mean = jnp.mean(values, axis=-1, keepdims=True)
    centred = values - row_mean
    row_var = jnp.mean(centred * centred, axis=-1, keepdims=True)
    return (centred * lax.rsqrt(row_var + 1e-05) * gain_row).astype(BF16)


def dot(left, right):
    return jnp.dot(left, right, preferred_element_type=F32)


def kernel(
    rows,
    taps,
    lengths_ref,
    targets_hbm,
    mask_hbm,
    gain_hbm,
    depth_hbm,
    mel_hbm,
    stem_hbm,
    gate_hbm,
    back_hbm,
    head_hbm,
    error_ref,
    score_ref,
    targets_ref,
    mask_ref,
    gain_ref,
    depth_ref,
    mel_bf,
    mel_f32,
    stem_w,
    gate_a,
    gate_b,
    back_a,
    back_b,
    head_a,
    head_b,
    back_w,
    stem_out,
    normed,
    gated,
    swished,
    tap_rows,
    square,
    error_cols,
    seed_parts,
    seq_parts,
    send_sem,
    recv_sem,
    local_sem,
    mel_send,
    mel_recv,
    out_send,
    out_recv,
):
    x = lax.axis_index("seed")
    fsdp = lax.axis_index("fsdp")
    y, c = fsdp // CORES, lax.rem(fsdp, CORES)
    z = lax.axis_index("seq")
    place = (x, y, c, z)
    wide = rows + 2 * HALO
    channels = GROUP * GROUPS

    barrier = pltpu.get_barrier_semaphore()
    peers = [(lax.rem(x + d, X), fsdp, lax.rem(z + e, Z)) for d in range(X) for e in range(Z) if d or e]
    peers += [(x, lax.rem(y + d, Y) * CORES + c, z) for d in range(1, Y)]
    peers += [(x, y * CORES + 1 - c, z)]
    for peer in peers:
        pl.semaphore_signal(barrier, inc=1, device_id=peer, device_id_type=MESH)

    mel_rows = 4 * rows
    loads = [
        pltpu.make_async_copy(mel_hbm.at[0], mel_bf.at[:, pl.ds(LANES, mel_rows)], local_sem.at[10]),
        pltpu.make_async_copy(stem_hbm.at[0], stem_w, local_sem.at[11]),
        pltpu.make_async_copy(depth_hbm, depth_ref, local_sem.at[12]),
        pltpu.make_async_copy(targets_hbm, targets_ref, local_sem.at[13]),
        pltpu.make_async_copy(gain_hbm, gain_ref, local_sem.at[14]),
        pltpu.make_async_copy(mask_hbm, mask_ref, local_sem.at[15]),
    ]
    for load in loads:
        load.start()

    specs = []
    for group in range(GROUPS):
        specs.append((gate_hbm, GROUP * group, GROUP, gate_a.at[group], False))
        specs.append((gate_hbm, channels + GROUP * group, GROUP, gate_b.at[group], True))
    half = back_hbm.shape[2] // 2
    specs.append((back_hbm, 0, half, back_a, False))
    specs.append((back_hbm, half, half, back_b, True))
    quarter = head_hbm.shape[2] // 2
    specs.append((head_hbm, 0, quarter, head_a, False))
    specs.append((head_hbm, quarter, quarter, head_b, True))
    pieces = []
    for index, (source, start, width, dst, y_first) in enumerate(specs):
        own = source.at[0, :, pl.ds(start, width)]
        pieces.append(
            Piece(place, own, dst, send_sem.at[index], recv_sem.at[index], local_sem.at[index], y_first, index == 7)
        )
    pl.semaphore_wait(barrier, len(peers))
    halo = [
        pltpu.make_async_remote_copy(
            src_ref=mel_hbm.at[0, :, pl.ds(mel_rows - LANES, LANES)],
            dst_ref=mel_bf.at[:, pl.ds(0, LANES)],
            send_sem=mel_send.at[0],
            recv_sem=mel_recv.at[0],
            device_id=(x, fsdp, lax.rem(z + 1, Z)),
            device_id_type=MESH,
        ),
        pltpu.make_async_remote_copy(
            src_ref=mel_hbm.at[0, :, pl.ds(0, LANES)],
            dst_ref=mel_bf.at[:, pl.ds(LANES + mel_rows, LANES)],
            send_sem=mel_send.at[1],
            recv_sem=mel_recv.at[1],
            device_id=(x, fsdp, lax.rem(z + Z - 1, Z)),
            device_id_type=MESH,
        ),
    ]
    length = lengths_ref[0]
    blocks = rows // LANES

    def small():
        for load in loads:
            load.wait()
        tap_rows[...] = jnp.zeros_like(tap_rows)
        tap_rows[1 : 1 + taps, :] = depth_ref[0].astype(F32)
        square[...] = jnp.zeros_like(square)
        for b in range(blocks):
            square[b : b + 1, :] = targets_ref[0:1, b * LANES : (b + 1) * LANES].astype(F32)
        square[...] = square[...].T

    tiles = mel_rows // LANES + 2

    def upright(half):
        if half == 0:
            for copy in halo:
                copy.wait_recv()

        @pl.loop(half * (tiles // 2), (half + 1) * (tiles // 2))
        def _(part):
            r0 = pl.multiple_of(part * LANES, LANES)
            past = (z == Z - 1) & (part == tiles - 1)
            tile = jnp.where(past, 0.0, mel_bf[:, pl.ds(r0, LANES)].astype(F32))
            mel_f32[pl.ds(r0, LANES), :] = tile.T

    tall = wide // 3
    skip = LANES - 4 * HALO

    def stem(part):
        r0 = part * tall
        window = [mel_f32[pl.ds(skip + 4 * r0 + i, tall, stride=4), :] for i in range(8)]
        frames = jnp.concatenate(window, axis=1).astype(BF16)
        out = dot(frames, stem_w[...]).astype(BF16)
        stem_out[r0 : r0 + tall, :] = out
        normed[r0 : r0 + tall, :] = normalised(out.astype(F32), gain_ref[0, 0:1, :])

    def gate(group):
        for part in range(3):
            r0 = part * tall
            left = normed[pl.ds(r0, tall), :]
            value = dot(left, gate_a[group].reshape(-1, GROUP))
            control = dot(left, gate_b[group].reshape(-1, GROUP))
            position = z * rows - HALO + r0 + lax.broadcasted_iota(jnp.int32, (tall, 1), 0)
            live = jnp.where((position >= 0) & (position < length), 1.0, 0.0).astype(F32)
            result = (value * jax.nn.sigmoid(control) * live).astype(BF16).astype(F32)
            for k in range(GROUP // LANES):
                gated[k, pl.ds(r0, tall), :] = result[:, k * LANES : (k + 1) * LANES]

    def depthwise(group, first, last):
        size = 128

        @pl.loop(first, last)
        def _(part):
            r0 = pl.multiple_of(part * size, size)
            for k in range(GROUP // LANES):
                column = group * GROUP + k * LANES
                around = gated[k, pl.ds(r0, size + 32), :]
                total = jnp.zeros((size, LANES), F32)
                for s in range(8):
                    partial = None
                    for a in range(4):
                        if a == 0 and s == 0:
                            continue
                        term = around[8 * a : 8 * a + size + 8] * tap_rows[8 * a + s : 8 * a + s + 1, column : column + LANES]
                        partial = term if partial is None else partial + term
                    if s:
                        partial = pltpu.roll(partial, size + 8 - s, 0)
                    total = total + partial[:size]
                swished[pl.ds(r0, size), column : column + LANES] = jax.nn.silu(total).astype(BF16)

    def contiguous():
        error_cols[...] = jnp.zeros_like(error_cols)

        @pl.loop(0, 16)
        def _(part):
            r0 = pl.multiple_of(part * 48, 48)
            flat_a = back_a.at[part // 4, lax.rem(part // 2, 2), pl.ds(lax.rem(part, 2) * 4, 4)]
            flat_b = back_b.at[part // 4, lax.rem(part // 2, 2), pl.ds(lax.rem(part, 2) * 4, 4)]
            back_w[pl.ds(r0, 48), :half] = flat_a[...].astype(F32).reshape(48, half).astype(BF16)
            back_w[pl.ds(r0, 48), half:] = flat_b[...].astype(F32).reshape(48, half).astype(BF16)

    size = 4 * LANES

    def project():
        @pl.loop(0, rows // size)
        def _(part):
            r0 = pl.multiple_of(part * size, size)
            product = dot(swished[pl.ds(r0, size), :], back_w[...])
            after = stem_out[pl.ds(r0 + HALO, size), :].astype(F32) + product
            normed[pl.ds(r0, size), :] = normalised(after, gain_ref[0, 1:2, :])

    def scores():
        @pl.loop(0, rows // size)
        def _(part):
            r0 = pl.multiple_of(part * size, size)
            second = normed[pl.ds(r0, size), :]
            logits = jnp.concatenate(
                [dot(second, head_a[...].reshape(-1, quarter)), dot(second, head_b[...].reshape(-1, quarter))], axis=1
            )
            top = jnp.max(logits, axis=-1, keepdims=True)
            weight = jnp.exp(logits - top)
            posterior = weight * (1.0 / jnp.sum(weight, axis=-1, keepdims=True))
            token = lax.broadcasted_iota(jnp.int32, (LANES, 2 * quarter), 1).astype(F32)
            lane = lax.broadcasted_iota(jnp.int32, (LANES, LANES), 1)
            for k in range(size // LANES):
                here = lane == size // LANES * part + k
                target = jnp.sum(jnp.where(here, square[...], 0.0), axis=1, keepdims=True)
                onehot = jnp.where(token == target, 1.0, 0.0)
                differ = posterior[k * LANES : (k + 1) * LANES] - onehot
                norm = jnp.sqrt(jnp.sum(differ * differ, axis=-1, keepdims=True))
                error_cols[...] = jnp.where(here, norm, error_cols[...])

    steps = rows // 128 // 2
    work = {"misc": small, "reloc": contiguous, "finA": project, "finB": scores}
    for k in range(2):
        work["mel%d" % k] = functools.partial(upright, k)
    for k in range(3):
        work["stem%d" % k] = functools.partial(stem, k)
    for k in range(GROUPS):
        work["gate%d" % k] = functools.partial(gate, k)
        work["dw%da" % k] = functools.partial(depthwise, k, 0, steps)
        work["dw%db" % k] = functools.partial(depthwise, k, steps, 2 * steps)
    sent_halo = False
    for token in ORDER:
        if not isinstance(token, int):
            if not sent_halo:
                for copy in halo:
                    copy.start()
                sent_halo = True
            work[token]()
        else:
            pieces[token].step()

    block = lax.broadcasted_iota(jnp.int32, (blocks, LANES), 0)
    position = z * rows + block * LANES + lax.broadcasted_iota(jnp.int32, (blocks, LANES), 1)
    for b in range(blocks):
        square[b : b + 1, :] = mask_ref[0:1, b * LANES : (b + 1) * LANES].astype(F32)
    own = error_cols[...].T[:blocks] * jnp.where(position < length, 1.0, 0.0) * square[:blocks, :]
    seed_parts[x] = own
    seq_parts[x, z] = jnp.sum(own, axis=0, keepdims=True)
    copies = []
    for d in range(1, X):
        copies.append((seed_parts.at[x], (lax.rem(x + d, X), fsdp, z)))
    for e in (4, 3, 5, 2, 6, 1, 7, 0):
        for d in (2, 1, 3, 0):
            if d or e:
                copies.append((seq_parts.at[x, z], (lax.rem(x + d, X), fsdp, lax.rem(z + e, Z))))
    copies = [
        pltpu.make_async_remote_copy(
            src_ref=ref,
            dst_ref=ref,
            send_sem=out_send.at[k],
            recv_sem=out_recv.at[k],
            device_id=device,
            device_id_type=MESH,
        )
        for k, (ref, device) in enumerate(copies)
    ]
    for copy in copies:
        copy.start()
    for copy in copies[: X - 1]:
        copy.wait()
    frame_error = (seed_parts[0] + seed_parts[1] + seed_parts[2] + seed_parts[3]) / 4.0
    for b in range(blocks):
        error_ref[0:1, b * LANES : (b + 1) * LANES] = frame_error[b : b + 1]
    for copy in copies[X - 1 :]:
        copy.wait()
    total = jnp.sum(seq_parts[...].reshape(X * Z, LANES), axis=0, keepdims=True) / 4.0
    numerator = jnp.sum(total, axis=1, keepdims=True)
    score_ref[...] = numerator / jnp.full((1, 1), length, jnp.int32).astype(F32)

    for copy in halo:
        copy.wait_send()
    for piece in pieces:
        piece.finish()


def body(mel, lengths, targets, mask, stem_weight, gate_weight, back_weight, depth_weight, head_weight, gain):
    rows = targets.shape[1]
    taps, channels = depth_weight.shape[1:]
    width = stem_weight.shape[2]
    wide = rows + 2 * HALO
    mels = mel.shape[2]
    mel_rows = mel.shape[1] + 2 * LANES
    deep, thin = gate_weight.shape[1], back_weight.shape[1]
    vocab = head_weight.shape[2]
    vmem = pl.BlockSpec(memory_space=pltpu.VMEM)
    hbm = pl.BlockSpec(memory_space=pltpu.HBM)
    share = (Y, CORES, Z)
    blocks = rows // LANES
    flops = 2 * wide * width * (stem_weight.shape[1] + 2 * channels) + 2 * rows * width * (channels + vocab)
    error, score = pl.pallas_call(
        functools.partial(kernel, rows, taps),
        out_shape=(jax.ShapeDtypeStruct((1, rows), F32), jax.ShapeDtypeStruct((1, 1), F32)),
        in_specs=[pl.BlockSpec(memory_space=pltpu.SMEM)] + [hbm] * 9,
        out_specs=(vmem, vmem),
        scratch_shapes=[
            pltpu.VMEM(targets.shape, jnp.int32),
            pltpu.VMEM(mask.shape, jnp.int32),
            pltpu.VMEM(gain.shape, F32),
            pltpu.VMEM(depth_weight.shape, BF16),
            pltpu.VMEM((mels, mel_rows), BF16),
            pltpu.VMEM((mel_rows, mels), F32),
            pltpu.VMEM(stem_weight.shape[1:], BF16),
            pltpu.VMEM((GROUPS,) + share + (deep, GROUP), BF16),
            pltpu.VMEM((GROUPS,) + share + (deep, GROUP), BF16),
            pltpu.VMEM(share + (thin, width // 2), BF16),
            pltpu.VMEM(share + (thin, width // 2), BF16),
            pltpu.VMEM(share + (deep, vocab // 2), BF16),
            pltpu.VMEM(share + (deep, vocab // 2), BF16),
            pltpu.VMEM((channels, width), BF16),
            pltpu.VMEM((wide, width), BF16),
            pltpu.VMEM((wide, width), BF16),
            pltpu.VMEM((GROUP // LANES, wide, LANES), F32),
            pltpu.VMEM((rows, channels), BF16),
            pltpu.VMEM((32, channels), F32),
            pltpu.VMEM((LANES, LANES), F32),
            pltpu.VMEM((LANES, LANES), F32),
            pltpu.VMEM((X, blocks, LANES), F32),
            pltpu.VMEM((X, Z, 1, LANES), F32),
            pltpu.SemaphoreType.DMA((10, 11)),
            pltpu.SemaphoreType.DMA((10, 11)),
            pltpu.SemaphoreType.DMA((16,)),
            pltpu.SemaphoreType.DMA((2,)),
            pltpu.SemaphoreType.DMA((2,)),
            pltpu.SemaphoreType.DMA((X - 1 + X * Z - 1,)),
            pltpu.SemaphoreType.DMA((X - 1 + X * Z - 1,)),
        ],
        compiler_params=pltpu.CompilerParams(
            collective_id=0, has_side_effects=True, vmem_limit_bytes=64 << 20
        ),
        cost_estimate=pl.CostEstimate(flops=flops, bytes_accessed=20 << 20, transcendentals=4 << 20),
        name="el2n_scores",
    )(lengths, targets, mask, gain, depth_weight, jnp.swapaxes(mel, 1, 2), stem_weight, gate_weight, back_weight, head_weight)
    return error, score.reshape(1)


def solution(mesh):
    in_specs = (
        P("fsdp", "seq", None),
        P("fsdp"),
        P("fsdp", "seq"),
        P("fsdp", "seq"),
        P("seed", None, None),
        P("seed", ("fsdp", "seq"), None),
        P("seed", ("fsdp", "seq"), None),
        P("seed", None, None),
        P("seed", ("fsdp", "seq"), None),
        P("seed", None, None),
    )
    out_specs = (P("fsdp", "seq"), P("fsdp"))
    return jax.shard_map(body, mesh=mesh, in_specs=in_specs, out_specs=out_specs, check_vma=False)
```
